32 devices in a mesh: rep: 2 (over x), cand: 16 (over z, y, core).
Axes of the slice: x: 2, y: 2, z: 4, core: 2. Of those that a mesh axis runs over, the one named last changes fastest.
Arguments:
- layer_activations: bfloat16 [64, 2, 8192], P(('rep', 'cand')), parts along dimension 0, may hold values from -6 to 6
- entry_scaling_factor: bfloat16 [8192], replicated, may hold values from 0.5 to 2
- asker_matrix: bfloat16 [8192, 8192], P(None, 'cand'), may hold values from -0.0625 to 0.0625
- address_matrix: bfloat16 [8192, 1024], P(None, 'cand'), may hold values from -0.0625 to 0.0625
- content_matrix: bfloat16 [8192, 1024], P(None, 'cand'), may hold values from -0.0625 to 0.0625
- final_matrix: bfloat16 [8192, 8192], P('cand'), may hold values from -0.1875 to 0.1875
- candidate_memory_blocks: bfloat16 [4096, 8, 2048], P(('rep', 'cand')), parts along dimension 0, may hold values from -64 to 64
- winning_candidates: int32 [64], P('rep'), parts along dimension 0, may hold values from 0 to 63, as said below
- winner_chip_assignment: int32 [64], P('rep'), parts along dimension 0, may hold values from 0 to 15, as said below
- candidate_block_map: int32 [128, 32], P('rep'), parts along dimension 0, may hold values from 0 to 2047, as said below
- candidate_filled_extent: int32 [128], P('rep'), parts along dimension 0, may hold values from 1 to 256
Outputs:
- mixing_result: bfloat16 [64, 2, 8192], P(('rep', 'cand')), parts along dimension 0
- winner_memory_blocks: bfloat16 [64, 32, 8, 2048], P(('rep', 'cand')), parts along dimension 0
The draws below stay inside these ranges and needn't reach their ends.
There are 2 independent parts, one for each index of `rep`. The reference program is written for one: setup_inputs(seed, part) draws one part's arguments, and reference() takes and returns one part's arrays. A program takes and returns all parts, laid end to end along the dimension named above; an argument that names none is the same for every part. Nothing has to cross between parts.
Inputs may be any that keep to these rules, and one draw needn't show every extreme that they name: `winning_candidates`: 32 distinct ids. `winner_chip_assignment`: every device index appears exactly 2 times. `candidate_block_map`: every page id appears exactly once in the table; for every device s, the pages that s holds of survivors placed on device d number 4 for all d but two: for one d they number 2 * 4, for another none.
All inputs are finite; a program needn't handle non-finite values.
Results may differ from the reference program's by a relative error of at most 0.006.
The reference program's roundings to bfloat16 on the way count: a program that leaves them out, or rounds other values in their place, can miss the bound.
Values may be sent and summed in bfloat16 or wider, within the bound.
A program may use at most 128 MiB of HBM per device.

```python
import math
import jax
import jax.numpy as jnp
from jax import lax

EMBED_DIM = 8192
ASKER_UNITS = 64
KV_ATTN_UNITS = 8
ATTN_DIM = 128
KVW = 1024
KEPT_ON_CHIP = 2
PAGE = 8
BLOCKS_EACH = 32
CTX = 256
WINNER_NUMBER = 32
CANDIDATE_TOTAL = 64
SLOTS_DEV = 128
PAGE_SHARE = 4
N_CAND = 16


def shared_layout(key):
    key_order, key_place, key_cycle, key_source, key_slots, key_dead = jax.random.split(key, 6)
    candidate_ordering = jax.random.permutation(key_order, CANDIDATE_TOTAL).astype(jnp.int32)
    picked_entries = candidate_ordering[:WINNER_NUMBER]
    placed = jax.random.permutation(key_place, jnp.repeat(jnp.arange(N_CAND, dtype=jnp.int32), KEPT_ON_CHIP)).astype(jnp.int32)
    cycle_order = jax.random.permutation(key_cycle, N_CAND).astype(jnp.int32)
    follow = jnp.roll(cycle_order, -1)
    dev_ids = jnp.arange(N_CAND, dtype=jnp.int32)
    counts = PAGE_SHARE * (1 + jnp.where(dev_ids[None, :] == cycle_order[:, None], 1, 0) - jnp.where(dev_ids[None, :] == follow[:, None], 1, 0))
    running = jnp.cumsum(counts, axis=0)
    kept_dev = N_CAND * PAGE_SHARE
    place_ids = jnp.arange(kept_dev, dtype=jnp.int32)
    sources = jnp.sum(jnp.where(running.T[:, None, :] <= place_ids[None, :, None], 1, 0), axis=2).astype(jnp.int32)
    mixing = jax.random.randint(key_source, (N_CAND, kept_dev), 0, 1 << 20) * kept_dev + place_ids[None, :]
    sources = jnp.take_along_axis(sources, jnp.argsort(mixing, axis=1), axis=1)
    src_flat = sources.reshape(-1)
    entry_ids = jnp.arange(src_flat.shape[0], dtype=jnp.int32)
    sorted_pos = jnp.argsort(src_flat, stable=True)
    ranks = jnp.zeros_like(src_flat).at[sorted_pos].set(entry_ids - src_flat[sorted_pos] * kept_dev)
    slot_scores = jax.random.randint(key_slots, (N_CAND, SLOTS_DEV), 0, 1 << 20) * SLOTS_DEV + jnp.arange(SLOTS_DEV, dtype=jnp.int32)[None, :]
    slot_perm = jnp.argsort(slot_scores, axis=1).astype(jnp.int32)
    kept_pages = src_flat * SLOTS_DEV + slot_perm[src_flat, ranks]
    free_pages = (dev_ids[:, None] * SLOTS_DEV + slot_perm[:, kept_dev:]).reshape(-1)
    permuted_entries = free_pages[jax.random.permutation(key_dead, free_pages.shape[0])]
    position_vector = jnp.arange(WINNER_NUMBER, dtype=jnp.int32)
    earlier = position_vector[None, :] < position_vector[:, None]
    same_dev = placed[None, :] == placed[:, None]
    position_on_chip = jnp.sum(jnp.where(earlier & same_dev, 1, 0), axis=1).astype(jnp.int32)
    lookup = placed[:, None] * kept_dev + position_on_chip[:, None] * BLOCKS_EACH + jnp.arange(BLOCKS_EACH, dtype=jnp.int32)[None, :]
    block_entries = jnp.zeros((CANDIDATE_TOTAL, BLOCKS_EACH), jnp.int32).at[picked_entries].set(kept_pages[lookup])
    block_entries = block_entries.at[candidate_ordering[WINNER_NUMBER:]].set(permuted_entries.reshape(CANDIDATE_TOTAL - WINNER_NUMBER, BLOCKS_EACH))
    return (picked_entries, placed, block_entries.astype(jnp.int32))


def draw_winning_candidates(key, part):
    layout = shared_layout(key)
    return layout[0]


def draw_winner_chip_assignment(key, part):
    layout = shared_layout(key)
    return layout[1]


def draw_candidate_block_map(key, part):
    layout = shared_layout(key)
    return layout[2]


def draw_candidate_memory_blocks(key, part):
    key = jax.random.fold_in(key, 7)
    key_base = jax.random.fold_in(key, 0)
    shape_all = (N_CAND * SLOTS_DEV, PAGE, 2 * KVW)
    values = jax.random.truncated_normal(key_base, -6.0, 6.0, shape_all, jnp.float32)
    return values.astype(jnp.bfloat16)


def set_ends(drawn, own_key, low, high):
    longest = drawn.shape.index(max(drawn.shape))
    spots = []
    for shift in (0, 1):
        where = [jax.random.randint(jax.random.fold_in(own_key, axis), (), 0, length) for axis, length in enumerate(drawn.shape)]
        where[longest] = (where[longest] + shift) % drawn.shape[longest]
        spots.append(tuple(where))
    return drawn.at[spots[0]].set(low).at[spots[1]].set(high)


def level_of(stream_key, dims, cuts, smallest, largest):
    def one(axis_at, shards_of):
        draws = jax.random.uniform(jax.random.fold_in(jax.random.fold_in(stream_key, 6), axis_at), (shards_of,), jnp.float32, smallest / len(cuts), largest / len(cuts))
        return jnp.repeat(jnp.exp(draws), dims[axis_at] // shards_of).reshape((-1,) + (1,) * (len(dims) - axis_at - 1))

    loudness = one(*cuts[0])
    for cut in cuts[1:]:
        loudness = loudness * one(*cut)
    return loudness


def normal_values(key, extent, scale, limit, cuts=(), held_as=jnp.bfloat16):
    result = jax.random.normal(key, extent, jnp.float32) * scale
    if len(cuts) > 0:
        result = level_of(key, extent, cuts, -0.22, 0.18) * result
    return jnp.clip(result, min=-limit, max=limit).astype(held_as)


def setup_inputs(seed: int = 0, part: int = 0) -> dict:
    arg_keys = jax.random.split(jax.random.key(seed), 12)
    own_keys = jax.random.split(jax.random.fold_in(arg_keys[11], part), 12)
    return {
        "layer_activations": normal_values(own_keys[0], (WINNER_NUMBER, 2, EMBED_DIM), 1.0, 6.0, ((0, 16),)),
        "entry_scaling_factor": jnp.clip(jnp.exp(jax.random.uniform(arg_keys[1], (EMBED_DIM,), jnp.float32, math.log(0.5), math.log(2.0))), 0.5, 2.0).astype(jnp.bfloat16),
        "asker_matrix": normal_values(arg_keys[2], (EMBED_DIM, ASKER_UNITS * ATTN_DIM), EMBED_DIM ** -0.5, 0.0625, ((1, 16),)),
        "address_matrix": normal_values(arg_keys[3], (EMBED_DIM, KVW), EMBED_DIM ** -0.5, 0.0625, ((1, 16),)),
        "content_matrix": normal_values(arg_keys[4], (EMBED_DIM, KVW), EMBED_DIM ** -0.5, 0.0625, ((1, 16),)),
        "final_matrix": normal_values(arg_keys[5], (ASKER_UNITS * ATTN_DIM, EMBED_DIM), (KV_ATTN_UNITS * ATTN_DIM) ** -0.5, 0.1875, ((0, 16),)),
        "candidate_memory_blocks": draw_candidate_memory_blocks(jax.random.fold_in(jax.random.fold_in(arg_keys[11], part), 71), part),
        "winning_candidates": draw_winning_candidates(jax.random.fold_in(jax.random.fold_in(arg_keys[11], part), 71), part),
        "winner_chip_assignment": draw_winner_chip_assignment(jax.random.fold_in(jax.random.fold_in(arg_keys[11], part), 71), part),
        "candidate_block_map": draw_candidate_block_map(jax.random.fold_in(jax.random.fold_in(arg_keys[11], part), 71), part),
        "candidate_filled_extent": set_ends(jax.random.randint(own_keys[10], (CANDIDATE_TOTAL,), 1, CTX + 1), jax.random.fold_in(own_keys[10], 1), 1, CTX).astype(jnp.int32),
    }


EPS = 1e-06
ROPE_BASE = 1000000.0
NEG_FILL = -1e+30

def spot_numbering(winner_chip_assignment, per_device):
    position_vector = jnp.arange(winner_chip_assignment.shape[0], dtype=jnp.int32)
    earlier = position_vector[None, :] < position_vector[:, None]
    same_dev = winner_chip_assignment[None, :] == winner_chip_assignment[:, None]
    position_on_chip = lax.optimization_barrier(jnp.sum(jnp.where(earlier & same_dev, 1, 0), axis=1)).astype(jnp.int32)
    return winner_chip_assignment * per_device + position_on_chip

def normalize(row_block, entry_scaling_factor):
    rows_f32 = row_block.astype(jnp.float32)
    mean_sq = lax.optimization_barrier(jnp.mean(rows_f32 * rows_f32, axis=-1, keepdims=True))
    return (rows_f32 * lax.rsqrt(mean_sq + EPS) * entry_scaling_factor.astype(jnp.float32)).astype(jnp.bfloat16)

def rotate(vectors, positions):
    half_dim = vectors.shape[-1] // 2
    frequencies = ROPE_BASE ** (-(jnp.arange(half_dim, dtype=jnp.float32) * 2.0 / vectors.shape[-1]))
    angles = positions.astype(jnp.float32)[..., None] * frequencies
    cosine_table = jnp.cos(angles)[..., None, :]
    sine_table = jnp.sin(angles)[..., None, :]
    first_half = vectors[..., :half_dim]
    second_half = vectors[..., half_dim:]
    return jnp.concatenate([first_half * cosine_table - second_half * sine_table, second_half * cosine_table + first_half * sine_table], axis=-1)

def attend(rotated_query, key_rot, arriving_contents, moved_blocks, context_extents):
    total_row_count = rotated_query.shape[0]
    heads_per_device = ASKER_UNITS // KV_ATTN_UNITS
    grouped_queries = rotated_query.astype(jnp.float32).reshape(total_row_count, 2, KV_ATTN_UNITS, heads_per_device, ATTN_DIM)
    stacked_pages = moved_blocks.reshape(total_row_count, -1, 2, KV_ATTN_UNITS, ATTN_DIM).astype(jnp.float32)
    cache_keys = stacked_pages[:, :, 0]
    cache_values = stacked_pages[:, :, 1]
    score_scale = 1.0 / math.sqrt(ATTN_DIM)
    scores_cache = jnp.einsum('btkgd,bskd->btkgs', grouped_queries, cache_keys) * score_scale
    scores_fresh = jnp.einsum('btkgd,bukd->btkgu', grouped_queries, key_rot.astype(jnp.float32)) * score_scale
    token_ids = jnp.arange(2, dtype=jnp.int32)
    valid_cache = (jnp.arange(stacked_pages.shape[1], dtype=jnp.int32)[None, :] < context_extents[:, None])[:, None, None, None, :]
    valid_fresh = (token_ids[None, :] <= token_ids[:, None])[None, :, None, None, :]
    masked_cache = jnp.where(valid_cache, scores_cache, NEG_FILL)
    masked_fresh = jnp.where(valid_fresh, scores_fresh, NEG_FILL)
    peak_score = jnp.maximum(lax.optimization_barrier(jnp.max(masked_cache, axis=-1, keepdims=True)), lax.optimization_barrier(jnp.max(masked_fresh, axis=-1, keepdims=True)))
    exp_cache = jnp.where(valid_cache, jnp.exp(masked_cache - peak_score), 0.0)
    exp_fresh = jnp.where(valid_fresh, jnp.exp(masked_fresh - peak_score), 0.0)
    denominator = lax.optimization_barrier(jnp.sum(exp_cache, axis=-1, keepdims=True)) + lax.optimization_barrier(jnp.sum(exp_fresh, axis=-1, keepdims=True))
    weights_cache = (exp_cache / denominator).astype(jnp.bfloat16).astype(jnp.float32)
    weights_fresh = (exp_fresh / denominator).astype(jnp.bfloat16).astype(jnp.float32)
    current_token_values = arriving_contents.astype(jnp.float32)
    combined_channels = jnp.einsum('btkgs,bskd->btkgd', weights_cache, cache_values) + jnp.einsum('btkgu,bukd->btkgd', weights_fresh, current_token_values)
    return combined_channels.reshape(total_row_count, 2, ASKER_UNITS * ATTN_DIM).astype(jnp.bfloat16)

def reference(layer_activations, entry_scaling_factor, asker_matrix, address_matrix, content_matrix, final_matrix, candidate_memory_blocks, winning_candidates, winner_chip_assignment, candidate_block_map, candidate_filled_extent):
    winner_placement_spot = spot_numbering(winner_chip_assignment, KEPT_ON_CHIP)
    rescaled_activations = normalize(layer_activations, entry_scaling_factor)
    merged_entries = rescaled_activations.reshape(WINNER_NUMBER * 2, EMBED_DIM)
    asker_vectors = jnp.dot(merged_entries, asker_matrix, preferred_element_type=jnp.float32).astype(jnp.bfloat16).reshape(WINNER_NUMBER, 2, ASKER_UNITS, ATTN_DIM)
    arriving_addresses = jnp.dot(merged_entries, address_matrix, preferred_element_type=jnp.float32).astype(jnp.bfloat16).reshape(WINNER_NUMBER, 2, KV_ATTN_UNITS, ATTN_DIM)
    arriving_contents = jnp.dot(merged_entries, content_matrix, preferred_element_type=jnp.float32).astype(jnp.bfloat16).reshape(WINNER_NUMBER, 2, KV_ATTN_UNITS, ATTN_DIM)
    context_extents = candidate_filled_extent[winning_candidates]
    positions = context_extents[:, None] + jnp.arange(2, dtype=jnp.int32)[None, :]
    rotated_query = rotate(asker_vectors.astype(jnp.float32), positions).astype(jnp.bfloat16)
    key_rot = rotate(arriving_addresses.astype(jnp.float32), positions).astype(jnp.bfloat16)
    moved_blocks = candidate_memory_blocks[candidate_block_map[winning_candidates]]
    combined_channels = attend(rotated_query, key_rot, arriving_contents, moved_blocks, context_extents)
    scaled_softmax_mixing = jnp.dot(combined_channels.reshape(WINNER_NUMBER * 2, ASKER_UNITS * ATTN_DIM), final_matrix, preferred_element_type=jnp.float32)
    scaled_softmax_mixing = scaled_softmax_mixing.reshape(WINNER_NUMBER, 2, EMBED_DIM).astype(jnp.bfloat16)
    mixing_result = jnp.zeros_like(scaled_softmax_mixing).at[winner_placement_spot].set(scaled_softmax_mixing)
    winner_memory_blocks = jnp.zeros_like(moved_blocks).at[winner_placement_spot].set(moved_blocks)
    return (mixing_result, winner_memory_blocks)
```

```python
import functools
import math

import jax
import jax.numpy as jnp
import numpy as np
from jax import lax
from jax.experimental import pallas as pl
from jax.experimental.pallas import tpu as pltpu
from jax.sharding import PartitionSpec as P

ASKER_UNITS = 64
KV_ATTN_UNITS = 8
ATTN_DIM = 128


EPS = 1e-06
ROPE_BASE = 1000000.0
NEG_FILL = -1e30


def spot_numbering(winner_chip_assignment, per_device):
    position_vector = jnp.arange(winner_chip_assignment.shape[0], dtype=jnp.int32)
    earlier = position_vector[None, :] < position_vector[:, None]
    same_dev = winner_chip_assignment[None, :] == winner_chip_assignment[:, None]
    position_on_chip = jnp.sum(jnp.where(earlier & same_dev, 1, 0), axis=1).astype(jnp.int32)
    return winner_chip_assignment * per_device + position_on_chip


def normalize(row_block, entry_scaling_factor):
    rows_f32 = row_block.astype(jnp.float32)
    mean_sq = jnp.mean(rows_f32 * rows_f32, axis=-1, keepdims=True)
    return (rows_f32 * lax.rsqrt(mean_sq + EPS) * entry_scaling_factor.astype(jnp.float32)).astype(
        jnp.bfloat16
    )


def rotate(vectors, positions):
    half_dim = vectors.shape[-1] // 2
    frequencies = ROPE_BASE ** (
        -(jnp.arange(half_dim, dtype=jnp.float32) * 2.0 / vectors.shape[-1])
    )
    angles = positions.astype(jnp.float32)[..., None] * frequencies
    cosine_table = jnp.cos(angles)[..., None, :]
    sine_table = jnp.sin(angles)[..., None, :]
    first_half = vectors[..., :half_dim]
    second_half = vectors[..., half_dim:]
    return jnp.concatenate(
        [
            first_half * cosine_table - second_half * sine_table,
            second_half * cosine_table + first_half * sine_table,
        ],
        axis=-1,
    )


ROWS = 16
MESH = pl.DeviceIdType.MESH
BF = jnp.bfloat16
F32 = jnp.float32


def place(z, y, core):
    return (z * 2 + y) * 2 + core


def remote(src, dst, send_sem, recv_sem, device):
    return pltpu.make_async_remote_copy(
        src_ref=src,
        dst_ref=dst,
        send_sem=send_sem,
        recv_sem=recv_sem,
        device_id={"cand": device},
        device_id_type=MESH,
    )


def greet_all(n, me):
    barrier = pltpu.get_barrier_semaphore()

    @pl.loop(1, n)
    def _(k):
        pl.semaphore_signal(
            barrier, inc=1, device_id={"cand": lax.rem(me + k, n)}, device_id_type=MESH
        )

    pl.semaphore_wait(barrier, n - 1)


class Gather:
    def __init__(self, n, me, own, buf, base, ss, rs):
        self.nz = n // 4
        self.core = lax.rem(me, 2)
        self.y = lax.rem(me // 2, 2)
        self.z = me // 4
        self.me, self.own, self.buf, self.base, self.ss, self.rs = me, own, buf, base, ss, rs

    def copy(self, src, block, level, k, device):
        dst = self.buf.at[self.base + block]
        return remote(
            dst if src is None else src, dst, self.ss.at[level, k], self.rs.at[level, k], device
        )

    def block(self, k, other_y, other_core):
        z = lax.rem(self.z - k + self.nz, self.nz)
        y = 1 - self.y if other_y else self.y
        core = 1 - self.core if other_core else self.core
        return place(z, y, core)

    def along_z(self, k):
        device = place(lax.rem(self.z + k, self.nz), self.y, self.core)
        return self.copy(self.own, self.me, 0, k, device)

    def across_y(self, k):
        device = place(self.z, 1 - self.y, self.core)
        return self.copy(None, self.block(k, False, False), 1, k, device)

    def across_core(self, k, other_y):
        device = place(self.z, self.y, 1 - self.core)
        return self.copy(
            None, self.block(k, other_y, False), 2, k + (self.nz if other_y else 0), device
        )

    def start(self):
        @pl.loop(1, self.nz)
        def _(k):
            self.along_z(k).start()

    def finish(self):
        self.across_y(0).start()
        self.across_core(0, False).start()

        @pl.loop(1, self.nz)
        def _(k):
            self.copy(None, self.block(k, False, False), 0, k, self.me).wait_recv()
            self.across_y(k).start()
            self.across_core(k, False).start()

        @pl.loop(0, self.nz)
        def _(k):
            self.copy(None, self.block(k, True, False), 1, k, self.me).wait_recv()
            self.across_core(k, True).start()

        @pl.loop(0, self.nz)
        def _(k):
            self.copy(None, self.block(k, False, True), 2, k, self.me).wait_recv()
            self.copy(None, self.block(k, True, True), 2, k + self.nz, self.me).wait_recv()

    def drain(self):
        @pl.loop(1, self.nz)
        def _(k):
            self.along_z(k).wait_send()

        @pl.loop(0, self.nz)
        def _(k):
            self.across_y(k).wait_send()
            self.across_core(k, False).wait_send()
            self.across_core(k, True).wait_send()


def move_kernel(
    n, heads, pick, spread, x, send, wq_hbm, wk_hbm, wv_hbm, pages, qkv,
    xall, wq, wk, wv, outq, local,
    x_ss, x_rs, o_ss, o_rs, p_ss, p_rs, q_ss, q_rs,
):
    me = lax.axis_index("cand")
    loads = [
        pltpu.make_async_copy(a, b, local.at[i])
        for i, (a, b) in enumerate(((wq_hbm, wq), (wk_hbm, wk), (wv_hbm, wv)))
    ]
    for load in loads:
        load.start()
    own_page = pltpu.make_async_copy(send.at[me], pages.at[me], local.at[3])
    own_extra = pltpu.make_async_copy(send.at[n], pages.at[n + me], local.at[4])
    own_page.start()
    own_extra.start()
    xall[me] = x[...]
    greet_all(n, me)
    rows = Gather(n, me, x, xall, 0, x_ss, x_rs)
    extra = Gather(n, me, send.at[n], pages, n, o_ss, o_rs)
    rows.start()
    extra.start()

    def page_copy(k):
        device = lax.rem(me + k, n)
        return remote(send.at[device], pages.at[me], p_ss.at[k], p_rs.at[k], device)

    @pl.loop(1, n)
    def _(k):
        page_copy(k).start()

    rows.finish()
    for load in loads:
        load.wait()
    flat = xall[...].reshape(n * ROWS, xall.shape[2])
    depth = xall.shape[2]
    q_sum = jnp.zeros((n * 4, wq.shape[1]), F32)
    k_sum = jnp.zeros((n * 4, wk.shape[1]), F32)
    v_sum = jnp.zeros((n * 4, wv.shape[1]), F32)
    for c in range(4):
        xc = jnp.dot(pick[c], flat, preferred_element_type=F32).astype(BF)
        part = pl.ds(c * depth, depth)
        q_sum += jnp.dot(xc, wq[part, :], preferred_element_type=F32)
        k_sum += jnp.dot(xc, wk[part, :], preferred_element_type=F32)
        v_sum += jnp.dot(xc, wv[part, :], preferred_element_type=F32)
    q16 = q_sum.astype(BF)
    slab = jnp.zeros((n * ROWS, ATTN_DIM), F32)
    for h in range(heads):
        slab += jnp.dot(
            spread[h], q16[:, h * ATTN_DIM : (h + 1) * ATTN_DIM], preferred_element_type=F32
        )
    pad = ATTN_DIM - wk.shape[1] - wv.shape[1]
    parts = [k_sum, v_sum] + ([jnp.zeros((n * 4, pad), F32)] if pad else [])
    kv16 = jnp.concatenate(parts, axis=1).astype(BF)
    kv_slab = jnp.dot(spread[0], kv16, preferred_element_type=F32)
    outq[:, :ROWS, :] = slab.astype(BF).reshape(n, ROWS, ATTN_DIM)
    outq[:, ROWS:, :] = kv_slab.astype(BF).reshape(n, ROWS, ATTN_DIM)
    own_q = pltpu.make_async_copy(outq.at[me], qkv.at[me], local.at[5])
    own_q.start()

    def q_copy(k):
        device = lax.rem(me + k, n)
        return remote(outq.at[device], qkv.at[me], q_ss.at[k], q_rs.at[k], device)

    @pl.loop(1, n)
    def _(k):
        q_copy(k).start()

    own_extra.wait()
    extra.finish()

    @pl.loop(1, n)
    def _(k):
        source = lax.rem(me - k + n, n)
        remote(send.at[0], pages.at[source], p_ss.at[k], p_rs.at[k], me).wait_recv()
        remote(outq.at[0], qkv.at[source], q_ss.at[k], q_rs.at[k], me).wait_recv()

    rows.drain()
    extra.drain()

    @pl.loop(1, n)
    def _(k):
        page_copy(k).wait_send()
        q_copy(k).wait_send()

    own_page.wait()
    own_q.wait()


def attend_kernel(
    n, heads, where_from, extents, pages, q, cos, sin, k_new, v_new, moved, mixed,
    held, scores, sems, out_sem,
):
    count = held.shape[0]

    def page_copy(i):
        return pltpu.make_async_copy(pages.at[where_from[i]], held.at[i], sems.at[i])

    @pl.loop(0, count)
    def _(i):
        page_copy(i).start()

    slabs = KV_ATTN_UNITS // heads
    rows = slabs * ROWS
    context = count * held.shape[1]
    half = context // 2
    row_c = lax.broadcasted_iota(jnp.int32, (rows, context), 0)
    col_c = lax.broadcasted_iota(jnp.int32, (rows, context), 1)
    survivor = (row_c % 4) // 2
    extent = jnp.where(survivor == 0, extents[0], extents[1])
    at = col_c - survivor * half
    valid_c = (at >= 0) & (at < extent)
    row_f = lax.broadcasted_iota(jnp.int32, (rows, ROWS), 0) % 4
    col_f = lax.broadcasted_iota(jnp.int32, (rows, ROWS), 1)
    valid_f = (col_f // 2 == row_f // 2) & (col_f % 2 <= row_f % 2) & (col_f < 4)
    scale = 1.0 / math.sqrt(ATTN_DIM)
    contract = (((1,), (1,)), ((), ()))

    @pl.loop(0, count)
    def _(i):
        page_copy(i).wait()

    out = pltpu.make_async_copy(held, moved, out_sem)
    out.start()
    for g in range(KV_ATTN_UNITS):
        qg = q[g * slabs : (g + 1) * slabs, :ROWS, :].astype(F32)
        qg = qg * cos[...][None] + pltpu.roll(qg, ATTN_DIM // 2, 2) * sin[...][None]
        qg = qg.reshape(rows, ATTN_DIM).astype(BF)
        lanes = pl.ds(g * ATTN_DIM, ATTN_DIM)
        keys = held[:, :, lanes].astype(F32).reshape(context, ATTN_DIM).astype(BF)
        lanes = pl.ds((KV_ATTN_UNITS + g) * ATTN_DIM, ATTN_DIM)
        values = held[:, :, lanes].astype(F32).reshape(context, ATTN_DIM).astype(BF)
        s_c = lax.dot_general(qg, keys, contract, preferred_element_type=F32) * scale
        s_f = lax.dot_general(qg, k_new[g], contract, preferred_element_type=F32) * scale
        s_c = jnp.where(valid_c, s_c, NEG_FILL)
        s_f = jnp.where(valid_f, s_f, NEG_FILL)
        peak = jnp.maximum(
            jnp.max(s_c, axis=-1, keepdims=True), jnp.max(s_f, axis=-1, keepdims=True)
        )
        e_c = jnp.where(valid_c, jnp.exp(s_c - peak), 0.0)
        e_f = jnp.where(valid_f, jnp.exp(s_f - peak), 0.0)
        total = jnp.sum(e_c, axis=-1, keepdims=True) + jnp.sum(e_f, axis=-1, keepdims=True)
        w_c = (e_c / total).astype(BF)
        w_f = (e_f / total).astype(BF)
        o = jnp.dot(w_c, values, preferred_element_type=F32)
        o += jnp.dot(w_f, v_new[g], preferred_element_type=F32)
        mixed[g * slabs : (g + 1) * slabs] = o.astype(BF).reshape(slabs, ROWS, ATTN_DIM)
    out.wait()


def project_kernel(
    n, heads, chunks, squeeze, mixed, wf_hbm, result,
    wf, gathered, partial, from_core, from_y, to_z, from_z, local,
    m_ss, m_rs, c_ss, c_rs, y_ss, y_rs, z_ss, z_rs,
):
    me = lax.axis_index("cand")
    nz = n // 4
    core, y, z = lax.rem(me, 2), lax.rem(me // 2, 2), me // 4
    load = pltpu.make_async_copy(wf_hbm, wf, local.at[0])
    load.start()
    gathered[me] = mixed[me]
    greet_all(n, me)

    def m_copy(k):
        device = lax.rem(me + k, n)
        return remote(mixed.at[device], gathered.at[me], m_ss.at[k], m_rs.at[k], device)

    @pl.loop(1, n)
    def _(k):
        m_copy(k).start()

    @pl.loop(1, n)
    def _(k):
        source = lax.rem(me - k + n, n)
        remote(mixed.at[0], gathered.at[source], m_ss.at[k], m_rs.at[k], me).wait_recv()

    flat = gathered[...].reshape(n * ROWS, ATTN_DIM)
    ordered = jnp.concatenate(
        [
            jnp.dot(squeeze[h], flat, preferred_element_type=F32).astype(BF)
            for h in range(heads)
        ],
        axis=1,
    )
    load.wait()
    width = wf.shape[1] // chunks

    def c_copy(i):
        return remote(
            partial.at[i, 1 - core], from_core.at[i], c_ss.at[i], c_rs.at[i], place(z, y, 1 - core)
        )

    def y_copy(i):
        return remote(
            partial.at[i, core, 1 - y], from_y.at[i], y_ss.at[i], y_rs.at[i],
            place(z, 1 - y, core),
        )

    def z_copy(i, k):
        other = lax.rem(z + k, nz)
        return remote(
            to_z.at[i, other], from_z.at[i, k], z_ss.at[i, k], z_rs.at[i, k],
            place(other, y, core),
        )

    for i in range(chunks):
        product = jnp.dot(
            ordered, wf[:, i * width : (i + 1) * width], preferred_element_type=F32
        )
        partial[i] = product.reshape(2, 2, nz * 4, width)
        c_copy(i).start()
    for i in range(chunks):
        c_copy(i).wait_recv()
        partial[i, core] = partial[i, core] + from_core[i]
        y_copy(i).start()
    for i in range(chunks):
        y_copy(i).wait_recv()
        total = partial[i, core, y] + from_y[i]
        for other in range(nz):
            to_z[i, other] = total[other * 4 : (other + 1) * 4, :]

        @pl.loop(1, nz)
        def _(k):
            z_copy(i, k).start()

    for i in range(chunks):
        total = to_z[i, z]
        for k in range(1, nz):
            z_copy(i, k).wait_recv()
            total = total + from_z[i, k]
        result[:, i * width : (i + 1) * width] = total.astype(BF)

    @pl.loop(1, n)
    def _(k):
        m_copy(k).wait_send()

    for i in range(chunks):
        c_copy(i).wait_send()
        y_copy(i).wait_send()

        @pl.loop(1, nz)
        def _(k):
            z_copy(i, k).wait_send()


def body(
    layer_activations,
    entry_scaling_factor,
    asker_matrix,
    address_matrix,
    content_matrix,
    final_matrix,
    candidate_memory_blocks,
    winning_candidates,
    winner_chip_assignment,
    candidate_block_map,
    candidate_filled_extent,
):
    n = lax.axis_size("cand")
    me = lax.axis_index("cand")
    nz = n // 4
    kept, tokens, embed = layer_activations.shape
    spots, page, page_width = candidate_memory_blocks.shape
    chain = candidate_block_map.shape[1]
    count = kept * chain
    share = count // n
    heads = asker_matrix.shape[1] // ATTN_DIM
    key_cols = address_matrix.shape[1]
    group_rows = kept * tokens

    slot = spot_numbering(winner_chip_assignment, kept)
    order = jnp.arange(slot.shape[0], dtype=jnp.int32)
    in_slot = slot[None, :] == order[:, None]
    keep = jnp.sum(jnp.where(in_slot, order[None, :], 0), axis=1)
    candidate = jnp.sum(jnp.where(in_slot, winning_candidates[None, :], 0), axis=1)
    table = candidate_block_map[candidate].reshape(n, count)
    extents = lax.dynamic_slice_in_dim(candidate_filled_extent[candidate], me * kept, kept)
    spot_ids = jnp.arange(count, dtype=jnp.int32)
    before = spot_ids[None, :] < spot_ids[:, None]
    mine = table // spots == me
    rank = jnp.sum(jnp.where(mine[:, None, :] & before[None], 1, 0), axis=2)
    ranks = jnp.arange(2 * share, dtype=jnp.int32)
    chosen = mine[:, None, :] & (rank[:, None, :] == ranks[None, :, None])
    sent = jnp.sum(jnp.where(chosen, (table % spots)[:, None, :], 0), axis=2)
    sent = jnp.concatenate(
        [sent[:, :share], jnp.sum(sent[:, share:], axis=0, keepdims=True)], axis=0
    )
    send = candidate_memory_blocks[sent.reshape(-1)].reshape(n + 1, share, page, page_width)
    arriving = lax.dynamic_slice_in_dim(table, me, 1)[0] // spots
    arrived_rank = jnp.sum(
        jnp.where((arriving[:, None] == arriving[None, :]) & before, 1, 0), axis=1
    )
    where_from = jnp.where(
        arrived_rank < share,
        arriving * share + arrived_rank,
        (n + arriving - 1) * share + arrived_rank,
    )

    x = normalize(layer_activations, entry_scaling_factor)
    pieces = ROWS // group_rows
    x = (
        x.reshape(group_rows, pieces, embed // pieces)
        .transpose(1, 0, 2)
        .reshape(ROWS, embed // pieces)
    )
    col = np.arange(n * ROWS)
    source_row = (col // ROWS) * group_rows + col % group_rows
    piece = (col // group_rows) % pieces
    wanted = (keep[:, None] * tokens + jnp.arange(tokens, dtype=jnp.int32)).reshape(-1)
    pick = jnp.where(
        (wanted[None, :, None] == source_row[None, None, :])
        & (np.arange(pieces)[:, None, None] == piece[None, None, :]),
        1.0,
        0.0,
    ).astype(BF)
    row = np.arange(n * group_rows)
    spread = np.stack(
        [(row[None, :] == source_row[:, None]) & (piece[:, None] == h) for h in range(pieces)]
    )
    by_level = (
        row.reshape(nz, 2, 2, group_rows).transpose(2, 1, 0, 3).reshape(-1)
    )
    squeeze = np.stack(
        [
            (by_level[:, None] == source_row[None, :]) & (piece[None, :] == h)
            for h in range(heads)
        ]
    )
    spread = jnp.asarray(spread.astype(jnp.bfloat16))
    squeeze = jnp.asarray(squeeze.astype(jnp.bfloat16))

    any_space = pl.BlockSpec(memory_space=pl.ANY)
    vmem = pl.BlockSpec(memory_space=pltpu.VMEM)
    smem = pl.BlockSpec(memory_space=pltpu.SMEM)
    dma = pltpu.SemaphoreType.DMA
    pages, qkv = pl.pallas_call(
        functools.partial(move_kernel, n, heads),
        out_shape=(
            jax.ShapeDtypeStruct((2 * n, share, page, page_width), BF),
            jax.ShapeDtypeStruct((n, 2 * ROWS, ATTN_DIM), BF),
        ),
        in_specs=[vmem, vmem, vmem] + [any_space] * 4,
        out_specs=(any_space, any_space),
        scratch_shapes=[
            pltpu.VMEM((n, ROWS, embed // pieces), BF),
            pltpu.VMEM(asker_matrix.shape, BF),
            pltpu.VMEM(address_matrix.shape, BF),
            pltpu.VMEM(content_matrix.shape, BF),
            pltpu.VMEM((n, 2 * ROWS, ATTN_DIM), BF),
            dma((6,)),
            dma((3, 2 * nz)),
            dma((3, 2 * nz)),
            dma((3, 2 * nz)),
            dma((3, 2 * nz)),
            dma((n,)),
            dma((n,)),
            dma((n,)),
            dma((n,)),
        ],
        compiler_params=pltpu.CompilerParams(
            collective_id=0, has_side_effects=True, vmem_limit_bytes=48 << 20
        ),
        name="move_and_project",
    )(pick, spread, x, send, asker_matrix, address_matrix, content_matrix)

    positions = extents[:, None] + jnp.arange(tokens, dtype=jnp.int32)[None, :]
    frequencies = ROPE_BASE ** (
        -(jnp.arange(ATTN_DIM // 2, dtype=jnp.float32) * 2.0 / ATTN_DIM)
    )
    angles = positions.reshape(-1).astype(F32)[:, None] * frequencies
    cosine, sine = jnp.cos(angles), jnp.sin(angles)
    cosine = jnp.concatenate([cosine, cosine], axis=1)
    sine = jnp.concatenate([-sine, sine], axis=1)
    fresh = qkv[:, ROWS : ROWS + group_rows, :]
    k_new = fresh[:, :, :key_cols].transpose(1, 0, 2).reshape(group_rows, KV_ATTN_UNITS, ATTN_DIM)
    v_new = fresh[:, :, key_cols : 2 * key_cols].transpose(1, 0, 2)
    v_new = v_new.reshape(group_rows, KV_ATTN_UNITS, ATTN_DIM)
    k_new = rotate(
        k_new.astype(F32).reshape(kept, tokens, KV_ATTN_UNITS, ATTN_DIM), positions
    ).astype(BF)
    k_new = k_new.reshape(group_rows, KV_ATTN_UNITS, ATTN_DIM).transpose(1, 0, 2)
    v_new = v_new.transpose(1, 0, 2)
    tall = ((0, 0), (0, ROWS - group_rows), (0, 0))
    k_new, v_new = jnp.pad(k_new, tall), jnp.pad(v_new, tall)

    moved, mixed = pl.pallas_call(
        functools.partial(attend_kernel, n, heads),
        out_shape=(
            jax.ShapeDtypeStruct((count, page, page_width), BF),
            jax.ShapeDtypeStruct((n, ROWS, ATTN_DIM), BF),
        ),
        in_specs=[smem, smem, any_space, vmem, vmem, vmem, vmem, vmem],
        out_specs=(any_space, vmem),
        scratch_shapes=[
            pltpu.VMEM((count, page, page_width), BF),
            pltpu.VMEM((8, 128), F32),
            dma((count,)),
            dma,
        ],
        compiler_params=pltpu.CompilerParams(vmem_limit_bytes=32 << 20),
        name="attend",
    )(
        where_from,
        extents,
        pages.reshape(2 * n * share, page, page_width),
        qkv,
        jnp.tile(cosine, (pieces, 1)),
        jnp.tile(sine, (pieces, 1)),
        k_new,
        v_new,
    )

    chunks = 4
    width = embed // chunks
    result = pl.pallas_call(
        functools.partial(project_kernel, n, heads, chunks),
        out_shape=jax.ShapeDtypeStruct((group_rows, embed), BF),
        in_specs=[vmem, vmem, any_space],
        out_specs=vmem,
        scratch_shapes=[
            pltpu.VMEM(final_matrix.shape, BF),
            pltpu.VMEM((n, ROWS, ATTN_DIM), BF),
            pltpu.VMEM((chunks, 2, 2, nz * group_rows, width), F32),
            pltpu.VMEM((chunks, 2, nz * group_rows, width), F32),
            pltpu.VMEM((chunks, nz * group_rows, width), F32),
            pltpu.VMEM((chunks, nz, group_rows, width), F32),
            pltpu.VMEM((chunks, nz, group_rows, width), F32),
            dma((1,)),
            dma((n,)),
            dma((n,)),
            dma((chunks,)),
            dma((chunks,)),
            dma((chunks,)),
            dma((chunks,)),
            dma((chunks, nz)),
            dma((chunks, nz)),
        ],
        compiler_params=pltpu.CompilerParams(
            collective_id=1, has_side_effects=True, vmem_limit_bytes=48 << 20
        ),
        name="project_and_sum",
    )(squeeze, mixed, final_matrix)
    return (
        result.reshape(kept, tokens, embed),
        moved.reshape(kept, chain, page, page_width),
    )


def solution(mesh):
    return jax.shard_map(
        body,
        mesh=mesh,
        in_specs=(
            P(("rep", "cand"), None, None),
            P(),
            P(None, "cand"),
            P(None, "cand"),
            P(None, "cand"),
            P("cand", None),
            P(("rep", "cand"), None, None),
            P("rep"),
            P("rep"),
            P("rep", None),
            P("rep"),
        ),
        out_specs=(P(("rep", "cand"), None, None), P(("rep", "cand"), None, None, None)),
        check_vma=False,
    )
```

```python
import functools
import math

import jax
import jax.numpy as jnp
import numpy as np
from jax import lax
from jax.experimental import pallas as pl
from jax.experimental.pallas import tpu as pltpu
from jax.sharding import PartitionSpec as P

ASKER_UNITS = 64
KV_ATTN_UNITS = 8
ATTN_DIM = 128


EPS = 1e-06
ROPE_BASE = 1000000.0
NEG_FILL = -1e30


def spot_numbering(winner_chip_assignment, per_device):
    position_vector = jnp.arange(winner_chip_assignment.shape[0], dtype=jnp.int32)
    earlier = position_vector[None, :] < position_vector[:, None]
    same_dev = winner_chip_assignment[None, :] == winner_chip_assignment[:, None]
    position_on_chip = jnp.sum(jnp.where(earlier & same_dev, 1, 0), axis=1).astype(jnp.int32)
    return winner_chip_assignment * per_device + position_on_chip


def normalize(row_block, entry_scaling_factor):
    rows_f32 = row_block.astype(jnp.float32)
    mean_sq = jnp.mean(rows_f32 * rows_f32, axis=-1, keepdims=True)
    return (rows_f32 * lax.rsqrt(mean_sq + EPS) * entry_scaling_factor.astype(jnp.float32)).astype(
        jnp.bfloat16
    )


def rotate(vectors, positions):
    half_dim = vectors.shape[-1] // 2
    frequencies = ROPE_BASE ** (
        -(jnp.arange(half_dim, dtype=jnp.float32) * 2.0 / vectors.shape[-1])
    )
    angles = positions.astype(jnp.float32)[..., None] * frequencies
    cosine_table = jnp.cos(angles)[..., None, :]
    sine_table = jnp.sin(angles)[..., None, :]
    first_half = vectors[..., :half_dim]
    second_half = vectors[..., half_dim:]
    return jnp.concatenate(
        [
            first_half * cosine_table - second_half * sine_table,
            second_half * cosine_table + first_half * sine_table,
        ],
        axis=-1,
    )


ROWS = 16
MESH = pl.DeviceIdType.MESH
BF = jnp.bfloat16
F32 = jnp.float32


def place(z, y, core):
    return (z * 2 + y) * 2 + core


def remote(src, dst, send_sem, recv_sem, device):
    return pltpu.make_async_remote_copy(
        src_ref=src,
        dst_ref=dst,
        send_sem=send_sem,
        recv_sem=recv_sem,
        device_id={"cand": device},
        device_id_type=MESH,
    )


def greet_all(n, me):
    barrier = pltpu.get_barrier_semaphore()

    @pl.loop(1, n)
    def _(k):
        pl.semaphore_signal(
            barrier, inc=1, device_id={"cand": lax.rem(me + k, n)}, device_id_type=MESH
        )

    pl.semaphore_wait(barrier, n - 1)


class Gather:
    def __init__(self, n, me, own, buf, base, ss, rs):
        self.nz = n // 4
        self.core = lax.rem(me, 2)
        self.y = lax.rem(me // 2, 2)
        self.z = me // 4
        self.me, self.own, self.buf, self.base, self.ss, self.rs = me, own, buf, base, ss, rs

    def copy(self, src, block, level, k, device):
        dst = self.buf.at[self.base + block]
        return remote(
            dst if src is None else src, dst, self.ss.at[level, k], self.rs.at[level, k], device
        )

    def block(self, k, other_y, other_core):
        z = lax.rem(self.z - k + self.nz, self.nz)
        y = 1 - self.y if other_y else self.y
        core = 1 - self.core if other_core else self.core
        return place(z, y, core)

    def along_z(self, k):
        device = place(lax.rem(self.z + k, self.nz), self.y, self.core)
        return self.copy(self.own, self.me, 0, k, device)

    def across_y(self, k):
        device = place(self.z, 1 - self.y, self.core)
        return self.copy(None, self.block(k, False, False), 1, k, device)

    def across_core(self, k, other_y):
        device = place(self.z, self.y, 1 - self.core)
        return self.copy(
            None, self.block(k, other_y, False), 2, k + (self.nz if other_y else 0), device
        )

    def start(self):
        @pl.loop(1, self.nz)
        def _(k):
            self.along_z(k).start()

    def finish(self):
        self.across_y(0).start()
        self.across_core(0, False).start()

        @pl.loop(1, self.nz)
        def _(k):
            self.copy(None, self.block(k, False, False), 0, k, self.me).wait_recv()
            self.across_y(k).start()
            self.across_core(k, False).start()

        @pl.loop(0, self.nz)
        def _(k):
            self.copy(None, self.block(k, True, False), 1, k, self.me).wait_recv()
            self.across_core(k, True).start()

        @pl.loop(0, self.nz)
        def _(k):
            self.copy(None, self.block(k, False, True), 2, k, self.me).wait_recv()
            self.copy(None, self.block(k, True, True), 2, k + self.nz, self.me).wait_recv()

    def drain(self):
        @pl.loop(1, self.nz)
        def _(k):
            self.along_z(k).wait_send()

        @pl.loop(0, self.nz)
        def _(k):
            self.across_y(k).wait_send()
            self.across_core(k, False).wait_send()
            self.across_core(k, True).wait_send()


def move_kernel(
    n, heads, sent, pick, spread, x, blocks_hbm, wq_hbm, wk_hbm, wv_hbm, pages, qkv,
    blocks, send, xall, wq, wk, wv, outq, local,
    x_ss, x_rs, o_ss, o_rs, p_ss, p_rs, q_ss, q_rs,
):
    me = lax.axis_index("cand")
    load_blocks = pltpu.make_async_copy(blocks_hbm, blocks, local.at[6])
    load_blocks.start()
    loads = [
        pltpu.make_async_copy(a, b, local.at[i])
        for i, (a, b) in enumerate(((wq_hbm, wq), (wk_hbm, wk), (wv_hbm, wv)))
    ]
    for load in loads:
        load.start()
    xall[me] = x[...]
    greet_all(n, me)
    rows = Gather(n, me, x, xall, 0, x_ss, x_rs)
    extra = Gather(n, me, send.at[n], pages, n, o_ss, o_rs)
    rows.start()
    load_blocks.wait()
    share = send.shape[1]

    def fill(row):
        for r in range(share):
            send[row, r] = blocks[sent[row * share + r]]

    def page_copy(k):
        device = lax.rem(me + k, n)
        return remote(send.at[device], pages.at[me], p_ss.at[k], p_rs.at[k], device)

    fill(n)
    own_extra = pltpu.make_async_copy(send.at[n], pages.at[n + me], local.at[4])
    own_extra.start()
    extra.start()

    @pl.loop(1, n)
    def _(k):
        fill(lax.rem(me + k, n))
        page_copy(k).start()

    fill(me)
    own_page = pltpu.make_async_copy(send.at[me], pages.at[me], local.at[3])
    own_page.start()
    rows.finish()
    for load in loads:
        load.wait()
    flat = xall[...].reshape(n * ROWS, xall.shape[2])
    depth = xall.shape[2]
    q_sum = jnp.zeros((n * 4, wq.shape[1]), F32)
    k_sum = jnp.zeros((n * 4, wk.shape[0]), F32)
    v_sum = jnp.zeros((n * 4, wv.shape[0]), F32)
    across = (((1,), (1,)), ((), ()))
    for c in range(4):
        xc = jnp.dot(pick[c], flat, preferred_element_type=F32).astype(BF)
        part = pl.ds(c * depth, depth)
        q_sum += jnp.dot(xc, wq[part, :], preferred_element_type=F32)
        k_sum += lax.dot_general(xc, wk[:, part], across, preferred_element_type=F32)
        v_sum += lax.dot_general(xc, wv[:, part], across, preferred_element_type=F32)
    q16 = q_sum.astype(BF)
    slab = jnp.zeros((n * ROWS, ATTN_DIM), F32)
    for h in range(heads):
        slab += jnp.dot(
            spread[h], q16[:, h * ATTN_DIM : (h + 1) * ATTN_DIM], preferred_element_type=F32
        )
    pad = ATTN_DIM - wk.shape[0] - wv.shape[0]
    parts = [k_sum, v_sum] + ([jnp.zeros((n * 4, pad), F32)] if pad else [])
    kv16 = jnp.concatenate(parts, axis=1).astype(BF)
    kv_slab = jnp.dot(spread[0], kv16, preferred_element_type=F32)
    outq[:, :ROWS, :] = slab.astype(BF).reshape(n, ROWS, ATTN_DIM)
    outq[:, ROWS:, :] = kv_slab.astype(BF).reshape(n, ROWS, ATTN_DIM)
    own_q = pltpu.make_async_copy(outq.at[me], qkv.at[me], local.at[5])
    own_q.start()

    def q_copy(k):
        device = lax.rem(me + k, n)
        return remote(outq.at[device], qkv.at[me], q_ss.at[k], q_rs.at[k], device)

    @pl.loop(1, n)
    def _(k):
        q_copy(k).start()

    own_extra.wait()
    extra.finish()

    @pl.loop(1, n)
    def _(k):
        source = lax.rem(me - k + n, n)
        remote(send.at[0], pages.at[source], p_ss.at[k], p_rs.at[k], me).wait_recv()
        remote(outq.at[0], qkv.at[source], q_ss.at[k], q_rs.at[k], me).wait_recv()

    rows.drain()
    extra.drain()

    @pl.loop(1, n)
    def _(k):
        page_copy(k).wait_send()
        q_copy(k).wait_send()

    own_page.wait()
    own_q.wait()


def attend_kernel(
    n, heads, where_from, extents, pages, q, cos, sin, k_new, v_new, moved, mixed,
    held, sems, out_sem,
):
    count = held.shape[0]

    def page_copy(i):
        return pltpu.make_async_copy(pages.at[where_from[i]], held.at[i], sems.at[i])

    @pl.loop(0, count)
    def _(i):
        page_copy(i).start()

    slabs = KV_ATTN_UNITS // heads
    rows = slabs * ROWS
    context = count * held.shape[1]
    half = context // 2
    row_c = lax.broadcasted_iota(jnp.int32, (rows, context), 0)
    col_c = lax.broadcasted_iota(jnp.int32, (rows, context), 1)
    survivor = (row_c % 4) // 2
    extent = jnp.where(survivor == 0, extents[0], extents[1])
    at = col_c - survivor * half
    valid_c = (at >= 0) & (at < extent)
    row_f = lax.broadcasted_iota(jnp.int32, (rows, ROWS), 0) % 4
    col_f = lax.broadcasted_iota(jnp.int32, (rows, ROWS), 1)
    valid_f = (col_f // 2 == row_f // 2) & (col_f % 2 <= row_f % 2) & (col_f < 4)
    scale = 1.0 / math.sqrt(ATTN_DIM)
    contract = (((1,), (1,)), ((), ()))

    @pl.loop(0, count)
    def _(i):
        page_copy(i).wait()

    out = pltpu.make_async_copy(held, moved, out_sem)
    out.start()
    for g in range(KV_ATTN_UNITS):
        qg = q[g * slabs : (g + 1) * slabs, :ROWS, :].astype(F32)
        qg = qg * cos[...][None] + pltpu.roll(qg, ATTN_DIM // 2, 2) * sin[...][None]
        qg = qg.reshape(rows, ATTN_DIM).astype(BF)
        lanes = pl.ds(g * ATTN_DIM, ATTN_DIM)
        keys = held[:, :, lanes].astype(F32).reshape(context, ATTN_DIM).astype(BF)
        lanes = pl.ds((KV_ATTN_UNITS + g) * ATTN_DIM, ATTN_DIM)
        values = held[:, :, lanes].astype(F32).reshape(context, ATTN_DIM).astype(BF)
        s_c = lax.dot_general(qg, keys, contract, preferred_element_type=F32) * scale
        s_f = lax.dot_general(qg, k_new[g], contract, preferred_element_type=F32) * scale
        s_c = jnp.where(valid_c, s_c, NEG_FILL)
        s_f = jnp.where(valid_f, s_f, NEG_FILL)
        peak = jnp.maximum(
            jnp.max(s_c, axis=-1, keepdims=True), jnp.max(s_f, axis=-1, keepdims=True)
        )
        e_c = jnp.where(valid_c, jnp.exp(s_c - peak), 0.0)
        e_f = jnp.where(valid_f, jnp.exp(s_f - peak), 0.0)
        total = jnp.sum(e_c, axis=-1, keepdims=True) + jnp.sum(e_f, axis=-1, keepdims=True)
        w_c = (e_c / total).astype(BF)
        w_f = (e_f / total).astype(BF)
        o = jnp.dot(w_c, values, preferred_element_type=F32)
        o += jnp.dot(w_f, v_new[g], preferred_element_type=F32)
        mixed[g * slabs : (g + 1) * slabs] = o.astype(BF).reshape(slabs, ROWS, ATTN_DIM)
    out.wait()


def project_kernel(
    n, heads, chunks, squeeze, mixed, wf_hbm, result,
    wf, gathered, partial, from_core, from_y, to_z, from_z, local,
    m_ss, m_rs, c_ss, c_rs, y_ss, y_rs, z_ss, z_rs,
):
    me = lax.axis_index("cand")
    nz = n // 4
    core, y, z = lax.rem(me, 2), lax.rem(me // 2, 2), me // 4
    load = pltpu.make_async_copy(wf_hbm, wf, local.at[0])
    load.start()
    gathered[me] = mixed[me]
    greet_all(n, me)

    def m_copy(k):
        device = lax.rem(me + k, n)
        return remote(mixed.at[device], gathered.at[me], m_ss.at[k], m_rs.at[k], device)

    @pl.loop(1, n)
    def _(k):
        m_copy(k).start()

    @pl.loop(1, n)
    def _(k):
        source = lax.rem(me - k + n, n)
        remote(mixed.at[0], gathered.at[source], m_ss.at[k], m_rs.at[k], me).wait_recv()

    flat = gathered[...].reshape(n * ROWS, ATTN_DIM)
    ordered = jnp.concatenate(
        [
            jnp.dot(squeeze[h], flat, preferred_element_type=F32).astype(BF)
            for h in range(heads)
        ],
        axis=1,
    )
    load.wait()
    width = wf.shape[1] // chunks

    def c_copy(i):
        return remote(
            partial.at[i, 1 - core], from_core.at[i], c_ss.at[i], c_rs.at[i], place(z, y, 1 - core)
        )

    def y_copy(i):
        return remote(
            partial.at[i, core, 1 - y], from_y.at[i], y_ss.at[i], y_rs.at[i],
            place(z, 1 - y, core),
        )

    def z_copy(i, k):
        other = lax.rem(z + k, nz)
        return remote(
            to_z.at[i, other], from_z.at[i, k], z_ss.at[i, k], z_rs.at[i, k],
            place(other, y, core),
        )

    for i in range(chunks):
        product = jnp.dot(
            ordered, wf[:, i * width : (i + 1) * width], preferred_element_type=F32
        )
        partial[i] = product.reshape(2, 2, nz * 4, width)
        c_copy(i).start()
    for i in range(chunks):
        c_copy(i).wait_recv()
        partial[i, core] = partial[i, core] + from_core[i]
        y_copy(i).start()
    for i in range(chunks):
        y_copy(i).wait_recv()
        total = partial[i, core, y] + from_y[i]
        for other in range(nz):
            to_z[i, other] = total[other * 4 : (other + 1) * 4, :]

        @pl.loop(1, nz)
        def _(k):
            z_copy(i, k).start()

    for i in range(chunks):
        total = to_z[i, z]
        for k in range(1, nz):
            z_copy(i, k).wait_recv()
            total = total + from_z[i, k]
        result[:, i * width : (i + 1) * width] = total.astype(BF)

    @pl.loop(1, n)
    def _(k):
        m_copy(k).wait_send()

    for i in range(chunks):
        c_copy(i).wait_send()
        y_copy(i).wait_send()

        @pl.loop(1, nz)
        def _(k):
            z_copy(i, k).wait_send()


def body(
    layer_activations,
    entry_scaling_factor,
    asker_matrix,
    address_matrix,
    content_matrix,
    final_matrix,
    candidate_memory_blocks,
    winning_candidates,
    winner_chip_assignment,
    candidate_block_map,
    candidate_filled_extent,
):
    n = lax.axis_size("cand")
    me = lax.axis_index("cand")
    nz = n // 4
    kept, tokens, embed = layer_activations.shape
    spots, page, page_width = candidate_memory_blocks.shape
    chain = candidate_block_map.shape[1]
    count = kept * chain
    share = count // n
    heads = asker_matrix.shape[1] // ATTN_DIM
    key_cols = address_matrix.shape[1]
    group_rows = kept * tokens

    slot = spot_numbering(winner_chip_assignment, kept)
    order = jnp.arange(slot.shape[0], dtype=jnp.int32)
    in_slot = slot[None, :] == order[:, None]
    keep = jnp.sum(jnp.where(in_slot, order[None, :], 0), axis=1)
    candidate = jnp.sum(jnp.where(in_slot, winning_candidates[None, :], 0), axis=1)
    table = candidate_block_map[candidate].reshape(n, count)
    extents = lax.dynamic_slice_in_dim(candidate_filled_extent[candidate], me * kept, kept)
    spot_ids = jnp.arange(count, dtype=jnp.int32)
    before = spot_ids[None, :] < spot_ids[:, None]
    mine = table // spots == me
    rank = jnp.sum(jnp.where(mine[:, None, :] & before[None], 1, 0), axis=2)
    ranks = jnp.arange(2 * share, dtype=jnp.int32)
    chosen = mine[:, None, :] & (rank[:, None, :] == ranks[None, :, None])
    sent = jnp.sum(jnp.where(chosen, (table % spots)[:, None, :], 0), axis=2)
    sent = jnp.concatenate(
        [sent[:, :share], jnp.sum(sent[:, share:], axis=0, keepdims=True)], axis=0
    )
    arriving = lax.dynamic_slice_in_dim(table, me, 1)[0] // spots
    arrived_rank = jnp.sum(
        jnp.where((arriving[:, None] == arriving[None, :]) & before, 1, 0), axis=1
    )
    where_from = jnp.where(
        arrived_rank < share,
        arriving * share + arrived_rank,
        (n + arriving - 1) * share + arrived_rank,
    )

    x = normalize(layer_activations, entry_scaling_factor)
    pieces = ROWS // group_rows
    x = (
        x.reshape(group_rows, pieces, embed // pieces)
        .transpose(1, 0, 2)
        .reshape(ROWS, embed // pieces)
    )
    col = np.arange(n * ROWS)
    source_row = (col // ROWS) * group_rows + col % group_rows
    piece = (col // group_rows) % pieces
    wanted = (keep[:, None] * tokens + jnp.arange(tokens, dtype=jnp.int32)).reshape(-1)
    pick = jnp.where(
        (wanted[None, :, None] == source_row[None, None, :])
        & (np.arange(pieces)[:, None, None] == piece[None, None, :]),
        1.0,
        0.0,
    ).astype(BF)
    row = np.arange(n * group_rows)
    spread = np.stack(
        [(row[None, :] == source_row[:, None]) & (piece[:, None] == h) for h in range(pieces)]
    )
    by_level = (
        row.reshape(nz, 2, 2, group_rows).transpose(2, 1, 0, 3).reshape(-1)
    )
    squeeze = np.stack(
        [
            (by_level[:, None] == source_row[None, :]) & (piece[None, :] == h)
            for h in range(heads)
        ]
    )
    spread = jnp.asarray(spread.astype(jnp.bfloat16))
    squeeze = jnp.asarray(squeeze.astype(jnp.bfloat16))

    any_space = pl.BlockSpec(memory_space=pl.ANY)
    vmem = pl.BlockSpec(memory_space=pltpu.VMEM)
    smem = pl.BlockSpec(memory_space=pltpu.SMEM)
    dma = pltpu.SemaphoreType.DMA
    pages, qkv = pl.pallas_call(
        functools.partial(move_kernel, n, heads),
        out_shape=(
            jax.ShapeDtypeStruct((2 * n, share, page, page_width), BF),
            jax.ShapeDtypeStruct((n, 2 * ROWS, ATTN_DIM), BF),
        ),
        in_specs=[smem, vmem, vmem, vmem] + [any_space] * 4,
        out_specs=(any_space, any_space),
        scratch_shapes=[
            pltpu.VMEM(candidate_memory_blocks.shape, BF),
            pltpu.VMEM((n + 1, share, page, page_width), BF),
            pltpu.VMEM((n, ROWS, embed // pieces), BF),
            pltpu.VMEM(asker_matrix.shape, BF),
            pltpu.VMEM(address_matrix.shape[::-1], BF),
            pltpu.VMEM(content_matrix.shape[::-1], BF),
            pltpu.VMEM((n, 2 * ROWS, ATTN_DIM), BF),
            dma((7,)),
            dma((3, 2 * nz)),
            dma((3, 2 * nz)),
            dma((3, 2 * nz)),
            dma((3, 2 * nz)),
            dma((n,)),
            dma((n,)),
            dma((n,)),
            dma((n,)),
        ],
        compiler_params=pltpu.CompilerParams(
            collective_id=0, has_side_effects=True, vmem_limit_bytes=48 << 20
        ),
        name="move_and_project",
    )(
        sent.reshape(-1),
        pick,
        spread,
        x,
        candidate_memory_blocks,
        asker_matrix,
        address_matrix.T,
        content_matrix.T,
    )

    positions = extents[:, None] + jnp.arange(tokens, dtype=jnp.int32)[None, :]
    frequencies = ROPE_BASE ** (
        -(jnp.arange(ATTN_DIM // 2, dtype=jnp.float32) * 2.0 / ATTN_DIM)
    )
    angles = positions.reshape(-1).astype(F32)[:, None] * frequencies
    cosine, sine = jnp.cos(angles), jnp.sin(angles)
    cosine = jnp.concatenate([cosine, cosine], axis=1)
    sine = jnp.concatenate([-sine, sine], axis=1)
    fresh = qkv[:, ROWS : ROWS + group_rows, :]
    k_new = fresh[:, :, :key_cols].transpose(1, 0, 2).reshape(group_rows, KV_ATTN_UNITS, ATTN_DIM)
    v_new = fresh[:, :, key_cols : 2 * key_cols].transpose(1, 0, 2)
    v_new = v_new.reshape(group_rows, KV_ATTN_UNITS, ATTN_DIM)
    k_new = rotate(
        k_new.astype(F32).reshape(kept, tokens, KV_ATTN_UNITS, ATTN_DIM), positions
    ).astype(BF)
    k_new = k_new.reshape(group_rows, KV_ATTN_UNITS, ATTN_DIM).transpose(1, 0, 2)
    v_new = v_new.transpose(1, 0, 2)
    tall = ((0, 0), (0, ROWS - group_rows), (0, 0))
    k_new, v_new = jnp.pad(k_new, tall), jnp.pad(v_new, tall)

    moved, mixed = pl.pallas_call(
        functools.partial(attend_kernel, n, heads),
        out_shape=(
            jax.ShapeDtypeStruct((count, page, page_width), BF),
            jax.ShapeDtypeStruct((n, ROWS, ATTN_DIM), BF),
        ),
        in_specs=[smem, smem, any_space, vmem, vmem, vmem, vmem, vmem],
        out_specs=(any_space, vmem),
        scratch_shapes=[
            pltpu.VMEM((count, page, page_width), BF),
            dma((count,)),
            dma,
        ],
        compiler_params=pltpu.CompilerParams(vmem_limit_bytes=32 << 20),
        name="attend",
    )(
        where_from,
        extents,
        pages.reshape(2 * n * share, page, page_width),
        qkv,
        jnp.tile(cosine, (pieces, 1)),
        jnp.tile(sine, (pieces, 1)),
        k_new,
        v_new,
    )

    chunks = 4
    width = embed // chunks
    result = pl.pallas_call(
        functools.partial(project_kernel, n, heads, chunks),
        out_shape=jax.ShapeDtypeStruct((group_rows, embed), BF),
        in_specs=[vmem, vmem, any_space],
        out_specs=vmem,
        scratch_shapes=[
            pltpu.VMEM(final_matrix.shape, BF),
            pltpu.VMEM((n, ROWS, ATTN_DIM), BF),
            pltpu.VMEM((chunks, 2, 2, nz * group_rows, width), F32),
            pltpu.VMEM((chunks, 2, nz * group_rows, width), F32),
            pltpu.VMEM((chunks, nz * group_rows, width), F32),
            pltpu.VMEM((chunks, nz, group_rows, width), F32),
            pltpu.VMEM((chunks, nz, group_rows, width), F32),
            dma((1,)),
            dma((n,)),
            dma((n,)),
            dma((chunks,)),
            dma((chunks,)),
            dma((chunks,)),
            dma((chunks,)),
            dma((chunks, nz)),
            dma((chunks, nz)),
        ],
        compiler_params=pltpu.CompilerParams(
            collective_id=1, has_side_effects=True, vmem_limit_bytes=48 << 20
        ),
        name="project_and_sum",
    )(squeeze, mixed, final_matrix)
    return (
        result.reshape(kept, tokens, embed),
        moved.reshape(kept, chain, page, page_width),
    )


def solution(mesh):
    return jax.shard_map(
        body,
        mesh=mesh,
        in_specs=(
            P(("rep", "cand"), None, None),
            P(),
            P(None, "cand"),
            P(None, "cand"),
            P(None, "cand"),
            P("cand", None),
            P(("rep", "cand"), None, None),
            P("rep"),
            P("rep"),
            P("rep", None),
            P("rep"),
        ),
        out_specs=(P(("rep", "cand"), None, None), P(("rep", "cand"), None, None, None)),
        check_vma=False,
    )
```

```python
import functools
import math

import jax
import jax.numpy as jnp
import numpy as np
from jax import lax
from jax.experimental import pallas as pl
from jax.experimental.pallas import tpu as pltpu
from jax.sharding import PartitionSpec as P

ASKER_UNITS = 64
KV_ATTN_UNITS = 8
ATTN_DIM = 128


EPS = 1e-06
ROPE_BASE = 1000000.0
NEG_FILL = -1e30


def spot_numbering(winner_chip_assignment, per_device):
    position_vector = jnp.arange(winner_chip_assignment.shape[0], dtype=jnp.int32)
    earlier = position_vector[None, :] < position_vector[:, None]
    same_dev = winner_chip_assignment[None, :] == winner_chip_assignment[:, None]
    position_on_chip = jnp.sum(jnp.where(earlier & same_dev, 1, 0), axis=1).astype(jnp.int32)
    return winner_chip_assignment * per_device + position_on_chip


def normalize(row_block, entry_scaling_factor):
    rows_f32 = row_block.astype(jnp.float32)
    mean_sq = jnp.mean(rows_f32 * rows_f32, axis=-1, keepdims=True)
    return (rows_f32 * lax.rsqrt(mean_sq + EPS) * entry_scaling_factor.astype(jnp.float32)).astype(
        jnp.bfloat16
    )


def rotate(vectors, positions):
    half_dim = vectors.shape[-1] // 2
    frequencies = ROPE_BASE ** (
        -(jnp.arange(half_dim, dtype=jnp.float32) * 2.0 / vectors.shape[-1])
    )
    angles = positions.astype(jnp.float32)[..., None] * frequencies
    cosine_table = jnp.cos(angles)[..., None, :]
    sine_table = jnp.sin(angles)[..., None, :]
    first_half = vectors[..., :half_dim]
    second_half = vectors[..., half_dim:]
    return jnp.concatenate(
        [
            first_half * cosine_table - second_half * sine_table,
            second_half * cosine_table + first_half * sine_table,
        ],
        axis=-1,
    )


ROWS = 16
MESH = pl.DeviceIdType.MESH
BF = jnp.bfloat16
F32 = jnp.float32


def place(z, y, core):
    return (z * 2 + y) * 2 + core


def remote(src, dst, send_sem, recv_sem, device):
    return pltpu.make_async_remote_copy(
        src_ref=src,
        dst_ref=dst,
        send_sem=send_sem,
        recv_sem=recv_sem,
        device_id={"cand": device},
        device_id_type=MESH,
    )


def greet_all(n, me):
    barrier = pltpu.get_barrier_semaphore()

    @pl.loop(1, n)
    def _(k):
        pl.semaphore_signal(
            barrier, inc=1, device_id={"cand": lax.rem(me + k, n)}, device_id_type=MESH
        )

    pl.semaphore_wait(barrier, n - 1)


class Gather:
    def __init__(self, n, me, own, buf, base, ss, rs):
        self.nz = n // 4
        self.core = lax.rem(me, 2)
        self.y = lax.rem(me // 2, 2)
        self.z = me // 4
        self.me, self.own, self.buf, self.base, self.ss, self.rs = me, own, buf, base, ss, rs

    def copy(self, src, block, level, k, device):
        dst = self.buf.at[self.base + block]
        return remote(
            dst if src is None else src, dst, self.ss.at[level, k], self.rs.at[level, k], device
        )

    def block(self, k, other_y, other_core):
        z = lax.rem(self.z - k + self.nz, self.nz)
        y = 1 - self.y if other_y else self.y
        core = 1 - self.core if other_core else self.core
        return place(z, y, core)

    def along_z(self, k):
        device = place(lax.rem(self.z + k, self.nz), self.y, self.core)
        return self.copy(self.own, self.me, 0, k, device)

    def across_y(self, k):
        device = place(self.z, 1 - self.y, self.core)
        return self.copy(None, self.block(k, False, False), 1, k, device)

    def across_core(self, k, other_y):
        device = place(self.z, self.y, 1 - self.core)
        return self.copy(
            None, self.block(k, other_y, False), 2, k + (self.nz if other_y else 0), device
        )

    def start(self):
        @pl.loop(1, self.nz)
        def _(k):
            self.along_z(k).start()

    def finish(self):
        self.across_y(0).start()
        self.across_core(0, False).start()

        @pl.loop(1, self.nz)
        def _(k):
            self.copy(None, self.block(k, False, False), 0, k, self.me).wait_recv()
            self.across_y(k).start()
            self.across_core(k, False).start()

        @pl.loop(0, self.nz)
        def _(k):
            self.copy(None, self.block(k, True, False), 1, k, self.me).wait_recv()
            self.across_core(k, True).start()

        @pl.loop(0, self.nz)
        def _(k):
            self.copy(None, self.block(k, False, True), 2, k, self.me).wait_recv()
            self.copy(None, self.block(k, True, True), 2, k + self.nz, self.me).wait_recv()

    def drain(self):
        @pl.loop(1, self.nz)
        def _(k):
            self.along_z(k).wait_send()

        @pl.loop(0, self.nz)
        def _(k):
            self.across_y(k).wait_send()
            self.across_core(k, False).wait_send()
            self.across_core(k, True).wait_send()


def move_kernel(
    n, heads, sent, pick, spread, x, blocks_hbm, wq_hbm, wk_hbm, wv_hbm, pages, qkv,
    blocks, send, xall, wq, wk, wv, outq, local,
    x_ss, x_rs, o_ss, o_rs, p_ss, p_rs, q_ss, q_rs,
):
    me = lax.axis_index("cand")
    load_blocks = pltpu.make_async_copy(blocks_hbm, blocks, local.at[6])
    load_blocks.start()
    loads = [
        pltpu.make_async_copy(a, b, local.at[i])
        for i, (a, b) in enumerate(((wq_hbm, wq), (wk_hbm, wk), (wv_hbm, wv)))
    ]
    for load in loads:
        load.start()
    xall[me] = x[...]
    greet_all(n, me)
    rows = Gather(n, me, x, xall, 0, x_ss, x_rs)
    extra = Gather(n, me, send.at[n], pages, n, o_ss, o_rs)
    rows.start()
    load_blocks.wait()
    share = send.shape[1]

    def fill(row):
        for r in range(share):
            send[row, r] = blocks[sent[row * share + r]]

    def page_copy(k):
        device = lax.rem(me + k, n)
        return remote(send.at[device], pages.at[me], p_ss.at[k], p_rs.at[k], device)

    fill(n)
    own_extra = pltpu.make_async_copy(send.at[n], pages.at[n + me], local.at[4])
    own_extra.start()
    extra.start()

    @pl.loop(1, n)
    def _(k):
        fill(lax.rem(me + k, n))
        page_copy(k).start()

    fill(me)
    own_page = pltpu.make_async_copy(send.at[me], pages.at[me], local.at[3])
    own_page.start()
    rows.finish()
    for load in loads:
        load.wait()
    flat = xall[...].reshape(n * ROWS, xall.shape[2])
    depth = xall.shape[2]
    q_sum = jnp.zeros((n * 4, wq.shape[1]), F32)
    k_sum = jnp.zeros((n * 4, wk.shape[0]), F32)
    v_sum = jnp.zeros((n * 4, wv.shape[0]), F32)
    across = (((1,), (1,)), ((), ()))
    for c in range(4):
        xc = jnp.dot(pick[c], flat, preferred_element_type=F32).astype(BF)
        part = pl.ds(c * depth, depth)
        q_sum += jnp.dot(xc, wq[part, :], preferred_element_type=F32)
        k_sum += lax.dot_general(xc, wk[:, part], across, preferred_element_type=F32)
        v_sum += lax.dot_general(xc, wv[:, part], across, preferred_element_type=F32)
    q16 = q_sum.astype(BF)
    slab = jnp.zeros((n * ROWS, ATTN_DIM), F32)
    for h in range(heads):
        slab += jnp.dot(
            spread[h], q16[:, h * ATTN_DIM : (h + 1) * ATTN_DIM], preferred_element_type=F32
        )
    pad = ATTN_DIM - wk.shape[0] - wv.shape[0]
    parts = [k_sum, v_sum] + ([jnp.zeros((n * 4, pad), F32)] if pad else [])
    kv16 = jnp.concatenate(parts, axis=1).astype(BF)
    kv_slab = jnp.dot(spread[0], kv16, preferred_element_type=F32)
    outq[:, :ROWS, :] = slab.astype(BF).reshape(n, ROWS, ATTN_DIM)
    outq[:, ROWS:, :] = kv_slab.astype(BF).reshape(n, ROWS, ATTN_DIM)
    own_q = pltpu.make_async_copy(outq.at[me], qkv.at[me], local.at[5])
    own_q.start()

    def q_copy(k):
        device = lax.rem(me + k, n)
        return remote(outq.at[device], qkv.at[me], q_ss.at[k], q_rs.at[k], device)

    @pl.loop(1, n)
    def _(k):
        q_copy(k).start()

    own_extra.wait()
    extra.finish()

    @pl.loop(1, n)
    def _(k):
        source = lax.rem(me - k + n, n)
        remote(send.at[0], pages.at[source], p_ss.at[k], p_rs.at[k], me).wait_recv()
        remote(outq.at[0], qkv.at[source], q_ss.at[k], q_rs.at[k], me).wait_recv()

    rows.drain()
    extra.drain()

    @pl.loop(1, n)
    def _(k):
        page_copy(k).wait_send()
        q_copy(k).wait_send()

    own_page.wait()
    own_q.wait()


def attend_kernel(
    n, heads, where_from, extents, pages, q, cos, sin, k_new, v_new, moved, mixed,
    held, sems, out_sem,
):
    count = held.shape[0]

    def page_copy(i):
        return pltpu.make_async_copy(pages.at[where_from[i]], held.at[i], sems.at[i])

    @pl.loop(0, count)
    def _(i):
        page_copy(i).start()

    slabs = KV_ATTN_UNITS // heads
    rows = slabs * ROWS
    context = count * held.shape[1]
    half = context // 2
    row_c = lax.broadcasted_iota(jnp.int32, (rows, context), 0)
    col_c = lax.broadcasted_iota(jnp.int32, (rows, context), 1)
    survivor = (row_c % 4) // 2
    extent = jnp.where(survivor == 0, extents[0], extents[1])
    at = col_c - survivor * half
    valid_c = (at >= 0) & (at < extent)
    row_f = lax.broadcasted_iota(jnp.int32, (rows, ROWS), 0) % 4
    col_f = lax.broadcasted_iota(jnp.int32, (rows, ROWS), 1)
    valid_f = (col_f // 2 == row_f // 2) & (col_f % 2 <= row_f % 2) & (col_f < 4)
    scale = 1.0 / math.sqrt(ATTN_DIM)
    contract = (((1,), (1,)), ((), ()))

    @pl.loop(0, count)
    def _(i):
        page_copy(i).wait()

    out = pltpu.make_async_copy(held, moved, out_sem)
    out.start()
    for g in range(KV_ATTN_UNITS):
        qg = q[g * slabs : (g + 1) * slabs, :ROWS, :].astype(F32)
        qg = qg * cos[...][None] + pltpu.roll(qg, ATTN_DIM // 2, 2) * sin[...][None]
        qg = qg.reshape(rows, ATTN_DIM).astype(BF)
        lanes = pl.ds(g * ATTN_DIM, ATTN_DIM)
        keys = held[:, :, lanes].astype(F32).reshape(context, ATTN_DIM).astype(BF)
        lanes = pl.ds((KV_ATTN_UNITS + g) * ATTN_DIM, ATTN_DIM)
        values = held[:, :, lanes].astype(F32).reshape(context, ATTN_DIM).astype(BF)
        s_c = lax.dot_general(qg, keys, contract, preferred_element_type=F32) * scale
        s_f = lax.dot_general(qg, k_new[g], contract, preferred_element_type=F32) * scale
        s_c = jnp.where(valid_c, s_c, NEG_FILL)
        s_f = jnp.where(valid_f, s_f, NEG_FILL)
        peak = jnp.maximum(
            jnp.max(s_c, axis=-1, keepdims=True), jnp.max(s_f, axis=-1, keepdims=True)
        )
        e_c = jnp.where(valid_c, jnp.exp(s_c - peak), 0.0)
        e_f = jnp.where(valid_f, jnp.exp(s_f - peak), 0.0)
        total = jnp.sum(e_c, axis=-1, keepdims=True) + jnp.sum(e_f, axis=-1, keepdims=True)
        w_c = (e_c / total).astype(BF)
        w_f = (e_f / total).astype(BF)
        o = jnp.dot(w_c, values, preferred_element_type=F32)
        o += jnp.dot(w_f, v_new[g], preferred_element_type=F32)
        mixed[g * slabs : (g + 1) * slabs] = o.astype(BF).reshape(slabs, ROWS, ATTN_DIM)
    out.wait()


def project_kernel(
    n, heads, chunks, squeeze, mixed, wf_hbm, result,
    wf, gathered, partial, from_core, from_y, to_z, from_z, local,
    m_ss, m_rs, c_ss, c_rs, y_ss, y_rs, z_ss, z_rs,
):
    me = lax.axis_index("cand")
    nz = n // 4
    core, y, z = lax.rem(me, 2), lax.rem(me // 2, 2), me // 4
    load = pltpu.make_async_copy(wf_hbm, wf, local.at[0])
    load.start()
    gathered[me] = mixed[me]
    greet_all(n, me)

    def m_copy(k):
        device = lax.rem(me + k, n)
        return remote(mixed.at[device], gathered.at[me], m_ss.at[k], m_rs.at[k], device)

    @pl.loop(1, n)
    def _(k):
        m_copy(k).start()

    @pl.loop(1, n)
    def _(k):
        source = lax.rem(me - k + n, n)
        remote(mixed.at[0], gathered.at[source], m_ss.at[k], m_rs.at[k], me).wait_recv()

    flat = gathered[...].reshape(n * ROWS, ATTN_DIM)
    ordered = jnp.concatenate(
        [
            jnp.dot(squeeze[h], flat, preferred_element_type=F32).astype(BF)
            for h in range(heads)
        ],
        axis=1,
    )
    load.wait()
    width = wf.shape[1] // chunks

    def c_copy(i):
        return remote(
            partial.at[i, 1 - core], from_core.at[i], c_ss.at[i], c_rs.at[i], place(z, y, 1 - core)
        )

    def y_copy(i):
        return remote(
            partial.at[i, core, 1 - y], from_y.at[i], y_ss.at[i], y_rs.at[i],
            place(z, 1 - y, core),
        )

    def z_copy(i, k):
        other = lax.rem(z + k, nz)
        return remote(
            to_z.at[i, other], from_z.at[i, k], z_ss.at[i, k], z_rs.at[i, k],
            place(other, y, core),
        )

    for i in range(chunks):
        product = jnp.dot(
            ordered, wf[:, i * width : (i + 1) * width], preferred_element_type=F32
        )
        partial[i] = product.reshape(2, 2, nz * 4, width)
        c_copy(i).start()
    for i in range(chunks):
        c_copy(i).wait_recv()
        partial[i, core] = partial[i, core] + from_core[i]
        y_copy(i).start()
    for i in range(chunks):
        y_copy(i).wait_recv()
        total = partial[i, core, y] + from_y[i]
        for other in range(nz):
            to_z[i, other] = total[other * 4 : (other + 1) * 4, :]

        @pl.loop(1, nz)
        def _(k):
            z_copy(i, k).start()

    for i in range(chunks):
        total = to_z[i, z]
        for k in range(1, nz):
            z_copy(i, k).wait_recv()
            total = total + from_z[i, k]
        result[:, i * width : (i + 1) * width] = total.astype(BF)

    @pl.loop(1, n)
    def _(k):
        m_copy(k).wait_send()

    for i in range(chunks):
        c_copy(i).wait_send()
        y_copy(i).wait_send()

        @pl.loop(1, nz)
        def _(k):
            z_copy(i, k).wait_send()


def body(
    layer_activations,
    entry_scaling_factor,
    asker_matrix,
    address_matrix,
    content_matrix,
    final_matrix,
    candidate_memory_blocks,
    winning_candidates,
    winner_chip_assignment,
    candidate_block_map,
    candidate_filled_extent,
):
    n = lax.axis_size("cand")
    me = lax.axis_index("cand")
    nz = n // 4
    kept, tokens, embed = layer_activations.shape
    spots, page, page_width = candidate_memory_blocks.shape
    chain = candidate_block_map.shape[1]
    count = kept * chain
    share = count // n
    heads = asker_matrix.shape[1] // ATTN_DIM
    key_cols = address_matrix.shape[1]
    group_rows = kept * tokens

    slot = spot_numbering(winner_chip_assignment, kept)
    order = jnp.arange(slot.shape[0], dtype=jnp.int32)
    in_slot = slot[None, :] == order[:, None]
    keep = jnp.sum(jnp.where(in_slot, order[None, :], 0), axis=1)
    candidate = jnp.sum(jnp.where(in_slot, winning_candidates[None, :], 0), axis=1)
    table = candidate_block_map[candidate].reshape(n, count)
    extents = lax.dynamic_slice_in_dim(candidate_filled_extent[candidate], me * kept, kept)
    spot_ids = jnp.arange(count, dtype=jnp.int32)
    before = spot_ids[None, :] < spot_ids[:, None]
    mine = table // spots == me
    rank = jnp.sum(jnp.where(mine[:, None, :] & before[None], 1, 0), axis=2)
    ranks = jnp.arange(2 * share, dtype=jnp.int32)
    chosen = mine[:, None, :] & (rank[:, None, :] == ranks[None, :, None])
    sent = jnp.sum(jnp.where(chosen, (table % spots)[:, None, :], 0), axis=2)
    sent = jnp.concatenate(
        [sent[:, :share], jnp.sum(sent[:, share:], axis=0, keepdims=True)], axis=0
    )
    arriving = lax.dynamic_slice_in_dim(table, me, 1)[0] // spots
    arrived_rank = jnp.sum(
        jnp.where((arriving[:, None] == arriving[None, :]) & before, 1, 0), axis=1
    )
    where_from = jnp.where(
        arrived_rank < share,
        arriving * share + arrived_rank,
        (n + arriving - 1) * share + arrived_rank,
    )

    x = normalize(layer_activations, entry_scaling_factor)
    pieces = ROWS // group_rows
    x = (
        x.reshape(group_rows, pieces, embed // pieces)
        .transpose(1, 0, 2)
        .reshape(ROWS, embed // pieces)
    )
    col = np.arange(n * ROWS)
    source_row = (col // ROWS) * group_rows + col % group_rows
    piece = (col // group_rows) % pieces
    wanted = (keep[:, None] * tokens + jnp.arange(tokens, dtype=jnp.int32)).reshape(-1)
    pick = jnp.where(
        (wanted[None, :, None] == source_row[None, None, :])
        & (np.arange(pieces)[:, None, None] == piece[None, None, :]),
        1.0,
        0.0,
    ).astype(BF)
    row = np.arange(n * group_rows)
    spread = np.stack(
        [(row[None, :] == source_row[:, None]) & (piece[:, None] == h) for h in range(pieces)]
    )
    by_level = (
        row.reshape(nz, 2, 2, group_rows).transpose(2, 1, 0, 3).reshape(-1)
    )
    squeeze = np.stack(
        [
            (by_level[:, None] == source_row[None, :]) & (piece[None, :] == h)
            for h in range(heads)
        ]
    )
    spread = jnp.asarray(spread.astype(jnp.bfloat16))
    squeeze = jnp.asarray(squeeze.astype(jnp.bfloat16))

    any_space = pl.BlockSpec(memory_space=pl.ANY)
    vmem = pl.BlockSpec(memory_space=pltpu.VMEM)
    smem = pl.BlockSpec(memory_space=pltpu.SMEM)
    dma = pltpu.SemaphoreType.DMA
    pages, qkv = pl.pallas_call(
        functools.partial(move_kernel, n, heads),
        out_shape=(
            jax.ShapeDtypeStruct((2 * n, share, page, page_width), BF),
            jax.ShapeDtypeStruct((n, 2 * ROWS, ATTN_DIM), BF),
        ),
        in_specs=[smem, vmem, vmem, vmem] + [any_space] * 4,
        out_specs=(any_space, any_space),
        scratch_shapes=[
            pltpu.VMEM(candidate_memory_blocks.shape, BF),
            pltpu.VMEM((n + 1, share, page, page_width), BF),
            pltpu.VMEM((n, ROWS, embed // pieces), BF),
            pltpu.VMEM(asker_matrix.shape, BF),
            pltpu.VMEM(address_matrix.shape[::-1], BF),
            pltpu.VMEM(content_matrix.shape[::-1], BF),
            pltpu.VMEM((n, 2 * ROWS, ATTN_DIM), BF),
            dma((7,)),
            dma((3, 2 * nz)),
            dma((3, 2 * nz)),
            dma((3, 2 * nz)),
            dma((3, 2 * nz)),
            dma((n,)),
            dma((n,)),
            dma((n,)),
            dma((n,)),
        ],
        compiler_params=pltpu.CompilerParams(
            collective_id=0, has_side_effects=True, vmem_limit_bytes=60 << 20
        ),
        name="move_and_project",
    )(
        sent.reshape(-1),
        pick,
        spread,
        x,
        candidate_memory_blocks,
        asker_matrix,
        address_matrix.T,
        content_matrix.T,
    )

    positions = extents[:, None] + jnp.arange(tokens, dtype=jnp.int32)[None, :]
    frequencies = ROPE_BASE ** (
        -(jnp.arange(ATTN_DIM // 2, dtype=jnp.float32) * 2.0 / ATTN_DIM)
    )
    angles = positions.reshape(-1).astype(F32)[:, None] * frequencies
    cosine, sine = jnp.cos(angles), jnp.sin(angles)
    cosine = jnp.concatenate([cosine, cosine], axis=1)
    sine = jnp.concatenate([-sine, sine], axis=1)
    fresh = qkv[:, ROWS : ROWS + group_rows, :]
    k_new = fresh[:, :, :key_cols].transpose(1, 0, 2).reshape(group_rows, KV_ATTN_UNITS, ATTN_DIM)
    v_new = fresh[:, :, key_cols : 2 * key_cols].transpose(1, 0, 2)
    v_new = v_new.reshape(group_rows, KV_ATTN_UNITS, ATTN_DIM)
    k_new = rotate(
        k_new.astype(F32).reshape(kept, tokens, KV_ATTN_UNITS, ATTN_DIM), positions
    ).astype(BF)
    k_new = k_new.reshape(group_rows, KV_ATTN_UNITS, ATTN_DIM).transpose(1, 0, 2)
    v_new = v_new.transpose(1, 0, 2)
    tall = ((0, 0), (0, ROWS - group_rows), (0, 0))
    k_new, v_new = jnp.pad(k_new, tall), jnp.pad(v_new, tall)

    moved, mixed = pl.pallas_call(
        functools.partial(attend_kernel, n, heads),
        out_shape=(
            jax.ShapeDtypeStruct((count, page, page_width), BF),
            jax.ShapeDtypeStruct((n, ROWS, ATTN_DIM), BF),
        ),
        in_specs=[smem, smem, any_space, vmem, vmem, vmem, vmem, vmem],
        out_specs=(any_space, vmem),
        scratch_shapes=[
            pltpu.VMEM((count, page, page_width), BF),
            dma((count,)),
            dma,
        ],
        compiler_params=pltpu.CompilerParams(vmem_limit_bytes=60 << 20),
        name="attend",
    )(
        where_from,
        extents,
        pages.reshape(2 * n * share, page, page_width),
        qkv,
        jnp.tile(cosine, (pieces, 1)),
        jnp.tile(sine, (pieces, 1)),
        k_new,
        v_new,
    )

    chunks = 4
    width = embed // chunks
    result = pl.pallas_call(
        functools.partial(project_kernel, n, heads, chunks),
        out_shape=jax.ShapeDtypeStruct((group_rows, embed), BF),
        in_specs=[vmem, vmem, any_space],
        out_specs=vmem,
        scratch_shapes=[
            pltpu.VMEM(final_matrix.shape, BF),
            pltpu.VMEM((n, ROWS, ATTN_DIM), BF),
            pltpu.VMEM((chunks, 2, 2, nz * group_rows, width), F32),
            pltpu.VMEM((chunks, 2, nz * group_rows, width), F32),
            pltpu.VMEM((chunks, nz * group_rows, width), F32),
            pltpu.VMEM((chunks, nz, group_rows, width), F32),
            pltpu.VMEM((chunks, nz, group_rows, width), F32),
            dma((1,)),
            dma((n,)),
            dma((n,)),
            dma((chunks,)),
            dma((chunks,)),
            dma((chunks,)),
            dma((chunks,)),
            dma((chunks, nz)),
            dma((chunks, nz)),
        ],
        compiler_params=pltpu.CompilerParams(
            collective_id=1, has_side_effects=True, vmem_limit_bytes=60 << 20
        ),
        name="project_and_sum",
    )(squeeze, mixed, final_matrix)
    return (
        result.reshape(kept, tokens, embed),
        moved.reshape(kept, chain, page, page_width),
    )


def solution(mesh):
    return jax.shard_map(
        body,
        mesh=mesh,
        in_specs=(
            P(("rep", "cand"), None, None),
            P(),
            P(None, "cand"),
            P(None, "cand"),
            P(None, "cand"),
            P("cand", None),
            P(("rep", "cand"), None, None),
            P("rep"),
            P("rep"),
            P("rep", None),
            P("rep"),
        ),
        out_specs=(P(("rep", "cand"), None, None), P(("rep", "cand"), None, None, None)),
        check_vma=False,
    )
```
